32 devices in a mesh: blk: 8 (over z, y), nbr: 4 (over x, core).
Axes of the slice: x: 2, y: 2, z: 4, core: 2. Of those that a mesh axis runs over, the one named last changes fastest.
Arguments:
- positions: float32 [3, 16384], P(None, ('blk', 'nbr')), may hold values from -6 to 6
- density: float32 [3, 16384], P(None, ('blk', 'nbr')), may hold values from -1.2 to 1.2
- upsample: float32 [32, 128], replicated, may hold values from -1 to 1
- cell_map: int32 [8, 4], P('blk'), may hold values from 0 to 3, as said below
- near_list: int32 [32, 12, 2], P(('blk', 'nbr')), may hold values from -1 to 15, as said below
Outputs:
- velocity: float32 [3, 16384], P(None, ('blk', 'nbr'))
The draws below stay inside these ranges and needn't reach their ends.
Inputs may be any that keep to these rules, and one draw needn't show every extreme that they name: Each row of cell_map is a permutation of the nbr indices. In near_list[c] every entry is either (-1, -1) or a pair (k, t) with t a cell id of c's row other than c's own; the pairs of one list are distinct; no cell id is named by more than 4 entries of one list, and in every row one cell is named by exactly 4 entries of every other cell's list.
All inputs are finite; a program needn't handle non-finite values.
Results may differ from the reference program's by a relative error of at most 0.0003.
Values sent between devices are 32-bit elements; how exact they have to be, the bound alone decides.
No kernel may reach another device: no remote copies, remote signals or barrier semaphores. Data moves between devices by JAX's collectives and lax.ppermute only.
A program may use at most 64 MiB of HBM per device.

```python
import math
import jax
import jax.numpy as jnp
from jax import lax

P_SIZE = 512
PANELS = 16
SLOTS = 4
PC = 32
PW = 128
CELLS = 32
NEAR = 12
N_BLK = 8
N_NBR = 4


def near_tables(key):
    map_keys = jax.random.split(jax.random.fold_in(key, 31), N_BLK)
    cell_table = jax.vmap(lambda sub_key: jax.random.permutation(sub_key, N_NBR))(map_keys).astype(jnp.int32)
    hub_cell = jax.random.randint(jax.random.fold_in(key, 32), (N_BLK,), 0, N_NBR)
    levels = jax.random.randint(jax.random.fold_in(key, 33), (N_BLK, N_NBR), 1, 9)
    levels = jnp.where(jnp.arange(N_NBR)[None, :] == hub_cell[:, None], 8, levels)
    return (cell_table, levels)


def draw_cell_map(key, part):
    return near_tables(key)[0]


def draw_near_list(key, part):
    cell_table, levels = near_tables(key)
    own_ids = jnp.argsort(cell_table, axis=1).astype(jnp.int32)
    offsets = jnp.arange(1, N_NBR, dtype=jnp.int32)
    targets = (own_ids[:, :, None] + offsets[None, None, :]) % N_NBR
    total_lists = N_BLK * N_NBR * (N_NBR - 1)
    panel_keys = jax.random.split(jax.random.fold_in(key, 34), total_lists)
    panel_draw = jax.vmap(lambda sub_key: jax.random.permutation(sub_key, PANELS)[:SLOTS])(panel_keys)
    panel_draw = panel_draw.reshape(N_BLK, N_NBR, N_NBR - 1, SLOTS).astype(jnp.int32)
    rolls = jax.random.randint(jax.random.fold_in(key, 35), (N_BLK, N_NBR, N_NBR - 1, SLOTS), 0, 8)
    target_level = levels[jnp.arange(N_BLK)[:, None, None], targets]
    keeping = rolls < target_level[..., None]
    target_full = jnp.broadcast_to(targets[..., None], (N_BLK, N_NBR, N_NBR - 1, SLOTS))
    panel_entry = jnp.where(keeping, panel_draw, -1)
    target_entry = jnp.where(keeping, target_full, -1)
    entries_all = jnp.stack([panel_entry, target_entry], axis=-1).reshape(N_BLK * N_NBR, NEAR, 2)
    order_keys = jax.random.split(jax.random.fold_in(key, 36), N_BLK * N_NBR)
    orders = jax.vmap(lambda sub_key: jax.random.permutation(sub_key, NEAR))(order_keys)
    entries_all = jnp.take_along_axis(entries_all, orders[:, :, None], axis=1)
    return entries_all.astype(jnp.int32)


def shard_levels(own_key, shape, pieces, least, top_value):
    def one(axis_at, blocks):
        draws = jax.random.uniform(jax.random.fold_in(jax.random.fold_in(own_key, 6), axis_at), (blocks,), jnp.float32, least / len(pieces), top_value / len(pieces))
        return jnp.repeat(jnp.exp(draws), shape[axis_at] // blocks).reshape((-1,) + (1,) * (len(shape) - axis_at - 1))

    loudness = one(*pieces[0])
    for cut in pieces[1:]:
        loudness = loudness * one(*cut)
    return loudness


def bell_draw(stream_key, dims, deviation, reach, pieces=(), kind=jnp.bfloat16):
    result = jax.random.normal(stream_key, dims, jnp.float32) * deviation
    if len(pieces) > 0:
        result = shard_levels(stream_key, dims, pieces, -0.22, 0.18) * result
    return jnp.clip(result, min=-reach, max=reach).astype(kind)


def setup_inputs(seed: int = 0) -> dict:
    arg_keys = jax.random.split(jax.random.key(seed), 6)
    positions = bell_draw(arg_keys[0], (3, CELLS * P_SIZE), 1.0, 6.0, ((1, 32),), jnp.float32)
    density = bell_draw(arg_keys[1], (3, CELLS * P_SIZE), 0.2, 1.2, ((1, 32),), jnp.float32)
    upsample = bell_draw(arg_keys[2], (PC, PW), PC ** -0.5, 1.0, (), jnp.float32)
    cell_map = draw_cell_map(jax.random.fold_in(arg_keys[5], 71), 0)
    near_list = draw_near_list(jax.random.fold_in(arg_keys[5], 71), 0)
    return {"positions": positions, "density": density, "upsample": upsample, "cell_map": cell_map, "near_list": near_list}


FAR_REG_SQ = 0.0625
NEAR_REG_SQ = 0.01
STOKES_COEF = 1.0 / (8.0 * math.pi)

def stokeslet(targets, sources, densities, reg_sq):
    offset_vec = targets[:, :, None] - sources[:, None, :]
    dist_sq = lax.optimization_barrier(jnp.sum(offset_vec * offset_vec, axis=0)) + reg_sq
    inv_cube = lax.rsqrt(dist_sq) / dist_sq
    leading = (dist_sq + reg_sq) * inv_cube
    projected = lax.optimization_barrier(jnp.sum(offset_vec * densities[:, None, :], axis=0)) * inv_cube
    first = lax.optimization_barrier(jnp.sum(leading[None] * densities[:, None, :], axis=-1))
    second = lax.optimization_barrier(jnp.sum(offset_vec * projected[None], axis=-1))
    return STOKES_COEF * (first + second)

def upsample_panels(panel_data, table):
    raised = jnp.einsum('kcp,pw->kcw', panel_data, table, precision=lax.Precision.HIGHEST)
    ratio = panel_data.shape[2] / table.shape[1]
    return jnp.concatenate([raised[:, :3], raised[:, 3:] * ratio], axis=1)

def reference(positions, density, upsample, cell_map, near_list):
    col_pos = positions.reshape(3, N_BLK, N_NBR, P_SIZE)
    col_den = density.reshape(3, N_BLK, N_NBR, P_SIZE)

    def column_far(column):
        tgt_pos = lax.dynamic_index_in_dim(col_pos, column, 2, keepdims=False)
        tgt_den = lax.dynamic_index_in_dim(col_den, column, 2, keepdims=False)
        targets = tgt_pos.reshape(3, N_BLK * P_SIZE)
        blocks = jnp.transpose(jnp.concatenate([tgt_pos, tgt_den], axis=0), (1, 0, 2))

        def add_block(summed, source_block):
            return (summed + stokeslet(targets, source_block[:3], source_block[3:], FAR_REG_SQ), None)
        summed, _ = lax.scan(add_block, jnp.zeros((3, N_BLK * P_SIZE), jnp.float32), blocks)
        return summed.reshape(3, N_BLK, P_SIZE)
    far_cols = lax.map(column_far, jnp.arange(N_NBR, dtype=jnp.int32))
    far_field = jnp.transpose(far_cols, (1, 2, 0, 3)).reshape(3, CELLS * P_SIZE)
    both = jnp.concatenate([positions, density], axis=0).reshape(6, CELLS, PANELS, PC)
    coarse = jnp.transpose(both, (1, 2, 0, 3)).reshape(CELLS * PANELS, 6, PC)
    fine_all = upsample_panels(coarse, upsample).reshape(CELLS, PANELS, 6, PW)
    lists = near_list.reshape(N_BLK, N_NBR, NEAR, 2)
    panel_ids = lists[..., 0]
    target_ids = lists[..., 1]
    is_valid = target_ids >= 0
    matches = target_ids[..., None] == jnp.arange(N_NBR, dtype=jnp.int32)
    dest_device = lax.optimization_barrier(jnp.sum(jnp.where(matches, cell_map[:, None, None, :], 0), axis=-1)).astype(jnp.int32)
    position = jnp.arange(NEAR, dtype=jnp.int32)
    earlier = (dest_device[..., :, None] == dest_device[..., None, :]) & is_valid[..., :, None] & is_valid[..., None, :] & (position[None, :] < position[:, None])
    rank_in_dest = lax.optimization_barrier(jnp.sum(earlier.astype(jnp.int32), axis=-1))
    slot_id = dest_device * SLOTS + rank_in_dest
    hits = (slot_id[..., None, :] == jnp.arange(N_NBR * SLOTS, dtype=jnp.int32)[:, None]) & is_valid[..., None, :]
    panel_at = lax.optimization_barrier(jnp.sum(jnp.where(hits, panel_ids[..., None, :], 0), axis=-1)).astype(jnp.int32)
    filled = jnp.any(hits, axis=-1)

    def near_cell(cell):
        row = cell // N_NBR
        column = cell % N_NBR
        ids = lax.dynamic_slice(panel_at, (row, jnp.int32(0), column * SLOTS), (1, N_NBR, SLOTS))[0]
        used = lax.dynamic_slice(filled, (row, jnp.int32(0), column * SLOTS), (1, N_NBR, SLOTS))[0]
        src_cells = row * N_NBR + jnp.arange(N_NBR, dtype=jnp.int32)[:, None]
        chosen = fine_all[src_cells, ids]
        chosen = jnp.where(used[:, :, None, None], chosen, jnp.zeros_like(chosen))
        flattened = jnp.transpose(chosen, (2, 0, 1, 3)).reshape(6, N_NBR * SLOTS * PW)
        targets = lax.dynamic_slice_in_dim(positions, cell * P_SIZE, P_SIZE, 1)
        return stokeslet(targets, flattened[:3], flattened[3:], NEAR_REG_SQ)
    near_cells = lax.map(near_cell, jnp.arange(CELLS, dtype=jnp.int32))
    near_field = jnp.transpose(near_cells, (1, 0, 2)).reshape(3, CELLS * P_SIZE)
    return far_field + near_field
```

```python
import functools
import math

import jax
import jax.numpy as jnp
from jax import lax
from jax.experimental import pallas as pl
from jax.experimental.pallas import tpu as pltpu
from jax.sharding import PartitionSpec as P

FAR_REG_SQ = 0.0625
NEAR_REG_SQ = 0.01
STOKES_COEF = 1.0 / (8.0 * math.pi)
F32 = jnp.float32
BF16 = jnp.bfloat16
LANES = 128
ROWS = 8
VMEM_LIMIT = 40 * 2**20


def split3(a):
    hi = a.astype(BF16).astype(F32)
    rest = a - hi
    mid = rest.astype(BF16).astype(F32)
    return hi, mid, rest - mid


def split2(a):
    hi = a.astype(BF16)
    return hi, (a - hi.astype(F32)).astype(BF16)


def stack_left(a):
    hi, mid, lo = split3(a)
    return jnp.concatenate([hi, hi, mid, mid, hi, lo], axis=0).astype(BF16)


def stack_right(a):
    hi, mid, lo = split3(a)
    return jnp.concatenate([hi, mid, hi, mid, lo, hi], axis=0).astype(BF16)


def stack_two(a):
    hi = a.astype(BF16).astype(F32)
    return jnp.concatenate([hi, a - hi], axis=0).astype(BF16)


def pad_rows(parts):
    have = sum(p.shape[0] for p in parts)
    return jnp.concatenate(parts + [jnp.zeros((ROWS - have, parts[0].shape[1]), F32)], axis=0)


def dot_first(a, b):
    return lax.dot_general(a, b, (((0,), (0,)), ((), ())), preferred_element_type=F32)


def dot(a, b):
    return jnp.dot(a, b, preferred_element_type=F32)


def target_features(x, reg_sq):
    inv = 1.0 / reg_sq
    ones = jnp.ones((1, x.shape[1]), F32)
    norm = jnp.sum(x * x, axis=0, keepdims=True) * inv
    dist = stack_right(pad_rows([(-2.0 * inv) * x, ones, norm]))
    return dist


def project_features(x):
    return stack_right(pad_rows([x, jnp.ones((1, x.shape[1]), F32)]))


def block_sum(source, dist_t, proj_t, reg_sq):
    inv = 1.0 / reg_sq
    inv_len = 1.0 / math.sqrt(reg_sq)
    y = source[0:3]
    f = source[3:6]
    ones = jnp.ones((1, y.shape[1]), F32)
    norm = jnp.sum(y * y, axis=0, keepdims=True) * inv + 1.0
    along = jnp.sum(y * f, axis=0, keepdims=True)
    dist_s = stack_left(pad_rows([y, norm, ones]))
    proj_s = stack_left(pad_rows([f, -along]))
    first = stack_two(pad_rows([f * inv_len]))
    second = stack_two(pad_rows([-y, ones]) * inv_len**3)
    root = lax.rsqrt(dot_first(dist_s, dist_t))
    cube = root * root * root
    lead_hi, lead_lo = split2(root + cube)
    q_hi, q_lo = split2(dot_first(proj_s, proj_t) * cube)
    return (dot(first, lead_hi) + dot(first, lead_lo)) + (dot(second, q_hi) + dot(second, q_lo))


def upsample_tiles(tiles, table):
    panel_pts, fine_pts = table.shape
    group = LANES // panel_pts
    zero = jnp.zeros((panel_pts, fine_pts), F32)
    spread = jnp.concatenate(
        [jnp.concatenate([table if h == g else zero for h in range(group)], axis=1) for g in range(group)], axis=0
    )
    t_hi, t_mid, t_lo = split3(jnp.concatenate(tiles, axis=0))
    w_hi, w_mid, w_lo = (w.astype(BF16) for w in split3(spread))
    n = t_hi.shape[0]
    on_hi = dot(jnp.concatenate([t_hi, t_mid, t_lo], axis=0).astype(BF16), w_hi)
    on_mid = dot(jnp.concatenate([t_hi, t_mid], axis=0).astype(BF16), w_mid)
    on_lo = dot(t_hi.astype(BF16), w_lo)
    fine = on_hi[0:n] + (on_hi[n : 2 * n] + on_mid[0:n]) + (on_hi[2 * n :] + on_mid[n:] + on_lo)
    ratio = panel_pts / fine_pts
    scale = jnp.where(lax.broadcasted_iota(jnp.int32, fine.shape, 0) % ROWS < 3, 1.0, ratio)
    fine = fine * scale
    return [fine[ROWS * i : ROWS * (i + 1)] for i in range(len(tiles))]


def pack_kernel(peers, slots, entries, panel_pts, pos_ref, den_ref, list_ref, map_ref, own_ref, *rest):
    tile_refs = rest[: peers - 1]
    table, count = rest[peers - 1 :]
    own_ref[0:3, :] = pos_ref[...]
    own_ref[3:6, :] = den_ref[...]
    own_ref[6:8, :] = jnp.zeros((2, own_ref.shape[1]), F32)
    me = lax.axis_index("nbr")

    def clear(i, _):
        table[i] = -1
        return 0

    lax.fori_loop(0, peers * slots + 1, clear, 0, unroll=True)
    for i in range(peers + 1):
        count[i] = 0

    def place(e, _):
        panel = list_ref[e, 0]
        cell = list_ref[e, 1]
        valid = cell >= 0
        dest = map_ref[0, jnp.maximum(cell, 0)]
        at = jnp.where(valid, dest, peers)
        rank = count[at]
        count[at] = rank + 1
        table[jnp.where(valid, dest * slots + rank, peers * slots)] = panel
        return 0

    lax.fori_loop(0, entries, place, 0, unroll=entries <= 16)
    group = LANES // panel_pts
    lane_group = lax.broadcasted_iota(jnp.int32, (ROWS, LANES), 1) // panel_pts
    for d in range(1, peers):
        dest = me ^ d
        tile = jnp.zeros((ROWS, LANES), F32)
        for s in range(slots):
            panel = table[dest * slots + s]
            safe = jnp.maximum(panel, 0)
            start = pl.multiple_of((safe // group) * LANES, LANES)
            piece = own_ref[:, pl.ds(start, LANES)]
            shift = (s - safe % group + group) % group * panel_pts
            moved = pltpu.roll(piece, shift, 1)
            tile = jnp.where((lane_group == s) & (panel >= 0), moved, tile)
        tile_refs[d - 1][...] = tile


def pack(positions, density, near_list, cell_map, panel_pts, peers):
    points = positions.shape[1]
    entries = near_list.shape[0]
    slots = LANES // panel_pts
    vmem = pl.BlockSpec(memory_space=pltpu.VMEM)
    smem = pl.BlockSpec(memory_space=pltpu.SMEM)
    return pl.pallas_call(
        functools.partial(pack_kernel, peers, slots, entries, panel_pts),
        out_shape=[jax.ShapeDtypeStruct((ROWS, points), F32)]
        + [jax.ShapeDtypeStruct((ROWS, LANES), F32)] * (peers - 1),
        in_specs=[vmem, vmem, smem, smem],
        out_specs=[vmem] * peers,
        scratch_shapes=[pltpu.SMEM((peers * slots + 1,), jnp.int32), pltpu.SMEM((peers + 1,), jnp.int32)],
        compiler_params=pltpu.CompilerParams(vmem_limit_bytes=VMEM_LIMIT),
        name="pack",
    )(positions, density, near_list, cell_map)


def sum_kernel(n_far, n_near, has_prior, final, *refs):
    refs = list(refs)
    x_ref = refs.pop(0)
    prior = refs.pop(0)[...] if has_prior else None
    far_refs = [refs.pop(0) for _ in range(n_far)]
    near_refs = [refs.pop(0) for _ in range(n_near)]
    table_ref = refs.pop(0) if n_near else None
    out_ref = refs.pop(0)
    x = x_ref[0:3, :]
    proj_t = project_features(x)
    total = jnp.zeros((2 * ROWS, x.shape[1]), F32)
    if n_far:
        dist_t = target_features(x, FAR_REG_SQ)
        for ref in far_refs:
            if len(ref.shape) == 2:
                total = total + block_sum(ref[...], dist_t, proj_t, FAR_REG_SQ)
            elif ref.shape[0] <= 4:
                for i in range(ref.shape[0]):
                    total = total + block_sum(ref[i], dist_t, proj_t, FAR_REG_SQ)
            else:
                total = lax.fori_loop(
                    0, ref.shape[0], lambda i, t, ref=ref: t + block_sum(ref[i], dist_t, proj_t, FAR_REG_SQ), total
                )
    if n_near:
        dist_t = target_features(x, NEAR_REG_SQ)
        for start in range(0, n_near, 3):
            for fine in upsample_tiles([r[...] for r in near_refs[start : start + 3]], table_ref[...]):
                total = total + block_sum(fine, dist_t, proj_t, NEAR_REG_SQ)
    summed = total[0:ROWS] + total[ROWS:]
    if has_prior:
        summed = summed + prior
    if final:
        out_ref[...] = STOKES_COEF * (summed[0:3] + x * summed[3:4])
    else:
        out_ref[...] = summed


def pair_sums(name, own, prior, far, near, table, final):
    points = own.shape[1]
    vmem = pl.BlockSpec(memory_space=pltpu.VMEM)
    args = [own] + ([prior] if prior is not None else []) + list(far) + list(near) + ([table] if near else [])
    pairs = points * (
        sum(a.size // ROWS for a in far) + (sum(a.size // ROWS for a in near) * table.shape[1] // table.shape[0] if near else 0)
    )
    return pl.pallas_call(
        functools.partial(sum_kernel, len(far), len(near), prior is not None, final),
        out_shape=jax.ShapeDtypeStruct((3 if final else ROWS, points), F32),
        in_specs=[vmem] * len(args),
        out_specs=vmem,
        compiler_params=pltpu.CompilerParams(vmem_limit_bytes=VMEM_LIMIT),
        cost_estimate=pl.CostEstimate(flops=300 * pairs, bytes_accessed=0, transcendentals=pairs),
        name=name,
    )(*args)


def flips(size, bit):
    return [(i, i ^ bit) for i in range(size)]


MODE = "B"


def shards(positions, density, upsample, cell_map, near_list):
    columns = lax.axis_size("blk")
    peers = lax.axis_size("nbr")
    own, *tiles = pack(positions, density, near_list[0], cell_map, upsample.shape[0], peers)
    if MODE == "B":
        bits = [b for b in (2, 4, 6) if b < columns]
        zs = [lax.ppermute(own, "blk", flips(columns, b)) for b in (6, 4, 2)]
        near = [lax.ppermute(t, "nbr", flips(peers, d + 1)) for d, t in enumerate(tiles)]
        part = pair_sums("own_far", own, None, [own], [], upsample, False)
        part = pair_sums("near", own, part, [], near, upsample, False)
        four = jnp.stack([own] + zs)
        other = lax.ppermute(four, "blk", flips(columns, 1))
        part = pair_sums("far_z", own, part, zs, [], upsample, False)
        rest = [other]
        bit = 8
        while bit < columns:
            both = jnp.concatenate([four, other]) if bit == 8 else jnp.concatenate([both, more])
            more = lax.ppermute(both, "blk", flips(columns, bit))
            rest.append(more)
            bit *= 2
        return pair_sums("far_y", own, part, rest, [], upsample, True)


def solution(mesh):
    placed = (
        P(None, ("blk", "nbr")),
        P(None, ("blk", "nbr")),
        P(),
        P("blk", None),
        P(("blk", "nbr"), None, None),
    )
    return jax.shard_map(
        shards, mesh=mesh, in_specs=placed, out_specs=P(None, ("blk", "nbr")), check_vma=False
    )
```

```python
import functools
import math

import jax
import jax.numpy as jnp
from jax import lax
from jax.experimental import pallas as pl
from jax.experimental.pallas import tpu as pltpu
from jax.sharding import PartitionSpec as P

FAR_REG_SQ = 0.0625
NEAR_REG_SQ = 0.01
STOKES_COEF = 1.0 / (8.0 * math.pi)
F32 = jnp.float32
BF16 = jnp.bfloat16
LANES = 128
ROWS = 8
VMEM_LIMIT = 40 * 2**20
WIDE = 1024
PACK_FLOPS = 900 * 10**6
PAIR_FLOPS = 3500


def split3(a):
    hi = a.astype(BF16).astype(F32)
    rest = a - hi
    mid = rest.astype(BF16).astype(F32)
    return hi, mid, rest - mid


def split2(a):
    hi = a.astype(BF16)
    return hi, (a - hi.astype(F32)).astype(BF16)


def stack_left(a):
    hi, mid, lo = split3(a)
    return jnp.concatenate([hi, hi, mid, mid, hi, lo], axis=0).astype(BF16)


def stack_right(a):
    hi, mid, lo = split3(a)
    return jnp.concatenate([hi, mid, hi, mid, lo, hi], axis=0).astype(BF16)


def stack_two(a):
    hi = a.astype(BF16).astype(F32)
    return jnp.concatenate([hi, a - hi], axis=0).astype(BF16)


def pad_rows(parts):
    have = sum(p.shape[0] for p in parts)
    return jnp.concatenate(parts + [jnp.zeros((ROWS - have, parts[0].shape[1]), F32)], axis=0)


def dot_first(a, b):
    return lax.dot_general(a, b, (((0,), (0,)), ((), ())), preferred_element_type=F32)


def dot(a, b):
    return jnp.dot(a, b, preferred_element_type=F32)


def target_features(x, reg_sq):
    inv = 1.0 / reg_sq
    ones = jnp.ones((1, x.shape[1]), F32)
    norm = jnp.sum(x * x, axis=0, keepdims=True) * inv
    dist = stack_right(pad_rows([(-2.0 * inv) * x, ones, norm]))
    return dist


def project_features(x):
    return stack_right(pad_rows([x, jnp.ones((1, x.shape[1]), F32)]))


def block_sum(source, dist_t, proj_t, reg_sq):
    inv = 1.0 / reg_sq
    inv_len = 1.0 / math.sqrt(reg_sq)
    y = source[0:3]
    f = source[3:6]
    ones = jnp.ones((1, y.shape[1]), F32)
    norm = jnp.sum(y * y, axis=0, keepdims=True) * inv + 1.0
    along = jnp.sum(y * f, axis=0, keepdims=True)
    dist_s = stack_left(pad_rows([y, norm, ones]))
    proj_s = stack_left(pad_rows([f, -along]))
    first = stack_two(pad_rows([f * inv_len]))
    second = stack_two(pad_rows([-y, ones]) * inv_len**3)
    root = lax.rsqrt(dot_first(dist_s, dist_t))
    cube = root * root * root
    lead_hi, lead_lo = split2(root + cube)
    q_hi, q_lo = split2(dot_first(proj_s, proj_t) * cube)
    return (dot(first, lead_hi) + dot(first, lead_lo)) + (dot(second, q_hi) + dot(second, q_lo))


def upsample_tiles(tiles, table):
    panel_pts, fine_pts = table.shape
    group = LANES // panel_pts
    zero = jnp.zeros((panel_pts, fine_pts), F32)
    spread = jnp.concatenate(
        [jnp.concatenate([table if h == g else zero for h in range(group)], axis=1) for g in range(group)], axis=0
    )
    t_hi, t_mid, t_lo = split3(jnp.concatenate(tiles, axis=0))
    w_hi, w_mid, w_lo = (w.astype(BF16) for w in split3(spread))
    n = t_hi.shape[0]
    on_hi = dot(jnp.concatenate([t_hi, t_mid, t_lo], axis=0).astype(BF16), w_hi)
    on_mid = dot(jnp.concatenate([t_hi, t_mid], axis=0).astype(BF16), w_mid)
    on_lo = dot(t_hi.astype(BF16), w_lo)
    fine = on_hi[0:n] + (on_hi[n : 2 * n] + on_mid[0:n]) + (on_hi[2 * n :] + on_mid[n:] + on_lo)
    ratio = panel_pts / fine_pts
    scale = jnp.where(lax.broadcasted_iota(jnp.int32, fine.shape, 0) % ROWS < 3, 1.0, ratio)
    fine = fine * scale
    return [fine[ROWS * i : ROWS * (i + 1)] for i in range(len(tiles))]


def pack_kernel(peers, slots, entries, panel_pts, own_ref, list_ref, map_ref, odd_ref, even_ref, table, count):
    me = lax.axis_index("nbr")
    for i in range(peers * slots + 1):
        table[i] = -1
    for i in range(peers + 1):
        count[i] = 0

    def place(e, _):
        panel = list_ref[0, 0, e]
        cell = list_ref[0, 1, e]
        valid = cell >= 0
        dest = map_ref[0, jnp.maximum(cell, 0)]
        at = jnp.where(valid, dest, peers)
        rank = count[at]
        count[at] = rank + 1
        table[jnp.where(valid, dest * slots + rank, peers * slots)] = panel
        return 0

    lax.fori_loop(0, entries, place, 0, unroll=entries <= 16)
    group = LANES // panel_pts
    lane_group = lax.broadcasted_iota(jnp.int32, (ROWS, LANES), 1) // panel_pts
    for d in range(1, peers):
        dest = me ^ d
        tile = jnp.zeros((ROWS, LANES), F32)
        for s in range(slots):
            panel = table[dest * slots + s]
            safe = jnp.maximum(panel, 0)
            start = pl.multiple_of((safe // group) * LANES, LANES)
            piece = own_ref[:, pl.ds(start, LANES)]
            shift = (s - safe % group + group) % group * panel_pts
            moved = pltpu.roll(piece, shift, 1)
            tile = jnp.where((lane_group == s) & (panel >= 0), moved, tile)
        if d % 2:
            odd_ref[d // 2] = tile
        else:
            even_ref[d // 2 - 1] = tile


def pack(own, near_list, cell_map, panel_pts, peers):
    entries = near_list.shape[2]
    slots = LANES // panel_pts
    vmem = pl.BlockSpec(memory_space=pltpu.VMEM)
    smem = pl.BlockSpec(memory_space=pltpu.SMEM)
    return pl.pallas_call(
        functools.partial(pack_kernel, peers, slots, entries, panel_pts),
        out_shape=[
            jax.ShapeDtypeStruct((peers // 2, ROWS, LANES), F32),
            jax.ShapeDtypeStruct((peers // 2 - 1, ROWS, LANES), F32),
        ],
        in_specs=[vmem, smem, smem],
        out_specs=[vmem] * 2,
        scratch_shapes=[pltpu.SMEM((peers * slots + 1,), jnp.int32), pltpu.SMEM((peers + 1,), jnp.int32)],
        compiler_params=pltpu.CompilerParams(vmem_limit_bytes=VMEM_LIMIT),
        cost_estimate=pl.CostEstimate(flops=PACK_FLOPS, bytes_accessed=0, transcendentals=0),
        name="pack",
    )(own, near_list, cell_map)


def wide_blocks(refs):
    singles = []
    for ref in refs:
        singles += [ref[...]] if len(ref.shape) == 2 else [ref[i] for i in range(ref.shape[0])]
    group = max(1, WIDE // singles[0].shape[1])
    return [jnp.concatenate(singles[i : i + group], axis=1) for i in range(0, len(singles), group)]


def sum_kernel(n_far, n_near, has_prior, keep, final, *refs):
    refs = list(refs)
    x_ref = refs.pop(0)
    prior = refs.pop(0)[...] if has_prior else None
    far_refs = [refs.pop(0) for _ in range(n_far)]
    near_refs = [refs.pop(0) for _ in range(n_near)]
    table_ref = refs.pop(0) if n_near else None
    out_ref = refs.pop(0)
    x = x_ref[0:3, :]
    proj_t = project_features(x)
    total = jnp.zeros((2 * ROWS, x.shape[1]), F32)
    if keep:
        at = 0
        for ref in far_refs:
            if len(ref.shape) == 2:
                refs[0][at] = ref[...]
                at += 1
            else:
                refs[0][at : at + ref.shape[0]] = ref[...]
                at += ref.shape[0]
    if n_far:
        dist_t = target_features(x, FAR_REG_SQ)
        small = [ref for ref in far_refs if len(ref.shape) == 2 or ref.shape[0] <= 4]
        if small:
            for block in wide_blocks(small):
                total = total + block_sum(block, dist_t, proj_t, FAR_REG_SQ)
        for ref in far_refs:
            if len(ref.shape) == 3 and ref.shape[0] > 4:
                total = lax.fori_loop(
                    0, ref.shape[0], lambda i, t, ref=ref: t + block_sum(ref[i], dist_t, proj_t, FAR_REG_SQ), total
                )
    if n_near:
        dist_t = target_features(x, NEAR_REG_SQ)
        tiles = []
        for ref in near_refs:
            tiles += [ref[i] for i in range(ref.shape[0])]
        for start in range(0, len(tiles), 3):
            fine = upsample_tiles(tiles[start : start + 3], table_ref[...])
            total = total + block_sum(jnp.concatenate(fine, axis=1), dist_t, proj_t, NEAR_REG_SQ)
    summed = total[0:ROWS] + total[ROWS:]
    if has_prior:
        summed = summed + prior
    if final:
        out_ref[...] = STOKES_COEF * (summed[0:3] + x * summed[3:4])
    else:
        out_ref[...] = summed


def pair_sums(name, own, prior, far, near, table, final=False, keep=False):
    points = own.shape[1]
    vmem = pl.BlockSpec(memory_space=pltpu.VMEM)
    args = [own] + ([prior] if prior is not None else []) + list(far) + list(near) + ([table] if near else [])
    far_sources = sum(a.size // ROWS for a in far)
    near_sources = sum(a.size // ROWS for a in near) * table.shape[1] // table.shape[0]
    pairs = points * (far_sources + near_sources)
    out_shape = [jax.ShapeDtypeStruct((3 if final else ROWS, points), F32)]
    if keep:
        out_shape.append(jax.ShapeDtypeStruct((far_sources // points, ROWS, points), F32))
    got = pl.pallas_call(
        functools.partial(sum_kernel, len(far), len(near), prior is not None, keep, final),
        out_shape=out_shape,
        in_specs=[vmem] * len(args),
        out_specs=[vmem] * len(out_shape),
        compiler_params=pltpu.CompilerParams(vmem_limit_bytes=VMEM_LIMIT),
        cost_estimate=pl.CostEstimate(flops=PAIR_FLOPS * pairs, bytes_accessed=0, transcendentals=pairs),
        name=name,
    )(*args)
    return got if keep else got[0]


def flips(size, bit):
    return [(i, i ^ bit) for i in range(size)]


def share_panels(odd, even):
    peers = lax.axis_size("nbr")
    held = {}
    for d in range(1, peers):
        held[d] = odd[d // 2] if d % 2 else even[d // 2 - 1]
    bit = 1
    while bit < peers:
        sent = [d for d in range(1, peers) if d & bit]
        stack = odd if bit == 1 else jnp.stack([held[d] for d in sent])
        got = lax.ppermute(stack, "nbr", flips(peers, bit))
        for i, d in enumerate(sent):
            held[d] = got[i]
        last = got
        bit *= 2
    done = [d for d in range(1, peers) if not d & (peers // 2)]
    return [last] + [held[d][None] for d in done]


ORDER = (4, 2, 6)


def shards(positions, density, upsample, cell_map, near_list):
    columns = lax.axis_size("blk")
    peers = lax.axis_size("nbr")
    own = jnp.concatenate([positions, density, jnp.zeros((2, positions.shape[1]), F32)], axis=0)
    zs = [lax.ppermute(own, "blk", flips(columns, b)) for b in ORDER]
    part = pair_sums("far_own", own, None, [own], [], upsample)
    odd, even = pack(own, jnp.swapaxes(near_list, 1, 2), cell_map, upsample.shape[0], peers)
    near = share_panels(odd, even)
    held = jnp.stack([own] + zs)
    bit = 1
    while bit < columns:
        got = lax.ppermute(held, "blk", flips(columns, bit))
        if bit == 1:
            part = pair_sums("far_z", own, part, zs, [], upsample)
            part = pair_sums("near", own, part, [], near, upsample)
            bit = 8
        else:
            part = pair_sums("far_%d" % bit, own, part, [last], [], upsample)
            bit *= 2
        held = jnp.concatenate([held, got])
        last = got
    return pair_sums("far_last", own, part, [last], [], upsample, final=True)


def solution(mesh):
    placed = (
        P(None, ("blk", "nbr")),
        P(None, ("blk", "nbr")),
        P(),
        P("blk", None),
        P(("blk", "nbr"), None, None),
    )
    return jax.shard_map(
        shards, mesh=mesh, in_specs=placed, out_specs=P(None, ("blk", "nbr")), check_vma=False
    )
```

```python
import functools
import math

import jax
import jax.numpy as jnp
from jax import lax
from jax.experimental import pallas as pl
from jax.experimental.pallas import tpu as pltpu
from jax.sharding import PartitionSpec as P

FAR_REG_SQ = 0.0625
NEAR_REG_SQ = 0.01
STOKES_COEF = 1.0 / (8.0 * math.pi)
F32 = jnp.float32
BF16 = jnp.bfloat16
LANES = 128
ROWS = 8
VMEM_LIMIT = 40 * 2**20
WIDE = 1536
USED = 6
FIRST = 1
SOON = 2
PACK_FLOPS = 900 * 10**6
PAIR_FLOPS = 3500


def split3(a):
    hi = a.astype(BF16).astype(F32)
    rest = a - hi
    mid = rest.astype(BF16).astype(F32)
    return hi, mid, rest - mid


def split2(a):
    hi = a.astype(BF16)
    return hi, (a - hi.astype(F32)).astype(BF16)


def stack_left(a):
    hi, mid, lo = split3(a)
    return jnp.concatenate([hi, hi, mid, mid, hi, lo], axis=0).astype(BF16)


def stack_right(a):
    hi, mid, lo = split3(a)
    return jnp.concatenate([hi, mid, hi, mid, lo, hi], axis=0).astype(BF16)


def stack_two(a):
    hi = a.astype(BF16).astype(F32)
    return jnp.concatenate([hi, a - hi], axis=0).astype(BF16)


def pad_rows(parts):
    have = sum(p.shape[0] for p in parts)
    return jnp.concatenate(parts + [jnp.zeros((ROWS - have, parts[0].shape[1]), F32)], axis=0)


def dot_first(a, b):
    return lax.dot_general(a, b, (((0,), (0,)), ((), ())), preferred_element_type=F32)


def dot(a, b):
    return jnp.dot(a, b, preferred_element_type=F32)


def target_features(x, reg_sq):
    inv = 1.0 / reg_sq
    ones = jnp.ones((1, x.shape[1]), F32)
    norm = jnp.sum(x * x, axis=0, keepdims=True) * inv
    dist = stack_right(pad_rows([(-2.0 * inv) * x, ones, norm]))
    return dist


def project_features(x):
    return stack_right(pad_rows([x, jnp.ones((1, x.shape[1]), F32)]))


def block_sum(source, dist_t, proj_t, reg_sq):
    inv = 1.0 / reg_sq
    inv_len = 1.0 / math.sqrt(reg_sq)
    y = source[0:3]
    f = source[3:6]
    ones = jnp.ones((1, y.shape[1]), F32)
    norm = jnp.sum(y * y, axis=0, keepdims=True) * inv + 1.0
    along = jnp.sum(y * f, axis=0, keepdims=True)
    dist_s = stack_left(pad_rows([y, norm, ones]))
    proj_s = stack_left(pad_rows([f, -along]))
    first = stack_two(pad_rows([f * inv_len]))
    second = stack_two(pad_rows([-y, ones]) * inv_len**3)
    root = lax.rsqrt(dot_first(dist_s, dist_t))
    cube = root * root * root
    lead_hi, lead_lo = split2(root + cube)
    q_hi, q_lo = split2(dot_first(proj_s, proj_t) * cube)
    return (dot(first, lead_hi) + dot(first, lead_lo)) + (dot(second, q_hi) + dot(second, q_lo))


def upsample_tiles(tiles, table):
    panel_pts, fine_pts = table.shape
    group = LANES // panel_pts
    zero = jnp.zeros((panel_pts, fine_pts), F32)
    spread = jnp.concatenate(
        [jnp.concatenate([table if h == g else zero for h in range(group)], axis=1) for g in range(group)], axis=0
    )
    t_hi, t_mid, t_lo = split3(jnp.concatenate(tiles, axis=0))
    w_hi, w_mid, w_lo = (w.astype(BF16) for w in split3(spread))
    n = t_hi.shape[0]
    on_hi = dot(jnp.concatenate([t_hi, t_mid, t_lo], axis=0).astype(BF16), w_hi)
    on_mid = dot(jnp.concatenate([t_hi, t_mid], axis=0).astype(BF16), w_mid)
    on_lo = dot(t_hi.astype(BF16), w_lo)
    fine = on_hi[0:n] + (on_hi[n : 2 * n] + on_mid[0:n]) + (on_hi[2 * n :] + on_mid[n:] + on_lo)
    ratio = panel_pts / fine_pts
    scale = jnp.where(lax.broadcasted_iota(jnp.int32, fine.shape, 0) % ROWS < 3, 1.0, ratio)
    fine = fine * scale
    return [fine[ROWS * i : ROWS * (i + 1)] for i in range(len(tiles))]


def pick_panels(peers, slots, panel_pts, own_ref, list_ref, map_ref, *rest):
    *tile_refs, table, count = rest
    entries = list_ref.shape[2]
    me = lax.axis_index("nbr")
    for i in range(peers * slots + 1):
        table[i] = -1
    for i in range(peers + 1):
        count[i] = 0

    def place(e, _):
        panel = list_ref[0, 0, e]
        cell = list_ref[0, 1, e]
        valid = cell >= 0
        dest = map_ref[0, jnp.maximum(cell, 0)]
        at = jnp.where(valid, dest, peers)
        rank = count[at]
        count[at] = rank + 1
        table[jnp.where(valid, dest * slots + rank, peers * slots)] = panel
        return 0

    lax.fori_loop(0, entries, place, 0, unroll=entries <= 16)
    group = LANES // panel_pts
    lane_group = lax.broadcasted_iota(jnp.int32, (ROWS, LANES), 1) // panel_pts
    for d in range(1, peers):
        dest = me ^ d
        tile = jnp.zeros((ROWS, LANES), F32)
        for s in range(slots):
            panel = table[dest * slots + s]
            safe = jnp.maximum(panel, 0)
            start = pl.multiple_of((safe // group) * LANES, LANES)
            piece = own_ref[:, pl.ds(start, LANES)]
            shift = (s - safe % group + group) % group * panel_pts
            moved = pltpu.roll(piece, shift, 1)
            tile = jnp.where((lane_group == s) & (panel >= 0), moved, tile)
        tile_refs[d - 1][0] = tile


def near_panels(own, near_list, cell_map, panel_pts, peers):
    slots = LANES // panel_pts
    vmem = pl.BlockSpec(memory_space=pltpu.VMEM)
    smem = pl.BlockSpec(memory_space=pltpu.SMEM)
    tile = jax.ShapeDtypeStruct((1, ROWS, LANES), F32)
    return pl.pallas_call(
        functools.partial(pick_panels, peers, slots, panel_pts),
        out_shape=[tile] * (peers - 1),
        in_specs=[vmem, smem, smem],
        out_specs=[vmem] * (peers - 1),
        scratch_shapes=[pltpu.SMEM((peers * slots + 1,), jnp.int32), pltpu.SMEM((peers + 1,), jnp.int32)],
        compiler_params=pltpu.CompilerParams(vmem_limit_bytes=VMEM_LIMIT),
        cost_estimate=pl.CostEstimate(flops=PACK_FLOPS, bytes_accessed=0, transcendentals=0),
        name="panels",
    )(own, near_list, cell_map)


def wide_blocks(refs):
    singles = []
    for ref in refs:
        if ref.shape[0] == ROWS:
            singles.append(ref[0:USED, :])
        else:
            singles += [ref[USED * i : USED * (i + 1), :] for i in range(ref.shape[0] // USED)]
    group = max(1, WIDE // singles[0].shape[1])
    return [jnp.concatenate(singles[i : i + group], axis=1) for i in range(0, len(singles), group)]


def sum_kernel(n_far, n_near, has_prior, final, *refs):
    refs = list(refs)
    x_ref = refs.pop(0)
    prior = refs.pop(0)[...] if has_prior else None
    far_refs = [refs.pop(0) for _ in range(n_far)]
    near_refs = [refs.pop(0) for _ in range(n_near)]
    table_ref = refs.pop(0) if n_near else None
    out_ref = refs.pop(0)
    x = x_ref[0:3, :]
    proj_t = project_features(x)
    total = jnp.zeros((2 * ROWS, x.shape[1]), F32)
    if n_far:
        dist_t = target_features(x, FAR_REG_SQ)
        for block in wide_blocks(far_refs):
            total = total + block_sum(block, dist_t, proj_t, FAR_REG_SQ)
    if n_near:
        dist_t = target_features(x, NEAR_REG_SQ)
        tiles = []
        for ref in near_refs:
            tiles += [ref[i] for i in range(ref.shape[0])]
        for start in range(0, len(tiles), 3):
            fine = upsample_tiles(tiles[start : start + 3], table_ref[...])
            total = total + block_sum(jnp.concatenate(fine, axis=1), dist_t, proj_t, NEAR_REG_SQ)
    summed = total[0:ROWS] + total[ROWS:]
    if has_prior:
        summed = summed + prior
    if final:
        out_ref[...] = STOKES_COEF * (summed[0:3] + x * summed[3:4])
    else:
        out_ref[...] = summed


def pair_sums(name, own, prior, far, near, table, final=False):
    points = own.shape[1]
    vmem = pl.BlockSpec(memory_space=pltpu.VMEM)
    args = [own] + ([prior] if prior is not None else []) + list(far) + list(near) + ([table] if near else [])
    far_sources = sum(a.size // ROWS for a in far)
    near_sources = sum(a.size // ROWS for a in near) * table.shape[1] // table.shape[0]
    pairs = points * (far_sources + near_sources)
    out_shape = [jax.ShapeDtypeStruct((3 if final else ROWS, points), F32)]
    got = pl.pallas_call(
        functools.partial(sum_kernel, len(far), len(near), prior is not None, final),
        out_shape=out_shape,
        in_specs=[vmem] * len(args),
        out_specs=[vmem] * len(out_shape),
        compiler_params=pltpu.CompilerParams(vmem_limit_bytes=VMEM_LIMIT),
        cost_estimate=pl.CostEstimate(flops=PAIR_FLOPS * pairs, bytes_accessed=0, transcendentals=pairs),
        name=name,
    )(*args)
    return got[0]


def place():
    blk = lax.axis_index("blk")
    first = blk < FIRST
    soon = jnp.logical_and(blk >= FIRST, blk < SOON * (lax.axis_size("blk") // 4))
    late = jnp.logical_and(blk >= FIRST, blk >= SOON * (lax.axis_size("blk") // 4))
    return first, soon, late


def far_total(x, blocks, part=None):
    total = jnp.zeros((2 * ROWS, x.shape[1]), F32)
    dist_t = target_features(x, FAR_REG_SQ)
    proj_t = project_features(x)
    for block in wide_blocks(blocks):
        total = total + block_sum(block, dist_t, proj_t, FAR_REG_SQ)
    total = total[0:ROWS] + total[ROWS:]
    return total if part is None else part + total


def first_kernel(own_ref, copy_ref, out_ref):
    first, soon, late = place()
    copy_ref[...] = own_ref[...]

    @pl.when(first)
    def _():
        out_ref[...] = far_total(own_ref[0:3, :], [own_ref])

    @pl.when(jnp.logical_not(first))
    def _():
        out_ref[...] = jnp.zeros(out_ref.shape, F32)


def before_kernel(own_ref, part_ref, *refs):
    *block_refs, held_ref, out_ref = refs
    first, soon, late = place()
    for i, ref in enumerate([own_ref, *block_refs]):
        held_ref[USED * i : USED * (i + 1), :] = ref[0:USED, :]

    @pl.when(first)
    def _():
        out_ref[...] = far_total(own_ref[0:3, :], block_refs[:1], part_ref[...])

    @pl.when(soon)
    def _():
        out_ref[...] = far_total(own_ref[0:3, :], [own_ref], part_ref[...])

    @pl.when(late)
    def _():
        out_ref[...] = part_ref[...]


def after_kernel(own_ref, part_ref, *refs):
    *block_refs, out_ref = refs
    first, soon, late = place()

    @pl.when(first)
    def _():
        out_ref[...] = far_total(own_ref[0:3, :], block_refs[1:], part_ref[...])

    @pl.when(soon)
    def _():
        out_ref[...] = far_total(own_ref[0:3, :], block_refs, part_ref[...])

    @pl.when(late)
    def _():
        out_ref[...] = far_total(own_ref[0:3, :], [own_ref, *block_refs], part_ref[...])


def far_first(own):
    vmem = pl.BlockSpec(memory_space=pltpu.VMEM)
    return pl.pallas_call(
        first_kernel,
        out_shape=[jax.ShapeDtypeStruct(own.shape, F32)] * 2,
        in_specs=[vmem],
        out_specs=[vmem] * 2,
        compiler_params=pltpu.CompilerParams(vmem_limit_bytes=VMEM_LIMIT),
        name="far_first",
    )(own)


def far_before(own, part, blocks):
    vmem = pl.BlockSpec(memory_space=pltpu.VMEM)
    return pl.pallas_call(
        before_kernel,
        out_shape=[
            jax.ShapeDtypeStruct((USED * (len(blocks) + 1), own.shape[1]), F32),
            jax.ShapeDtypeStruct(own.shape, F32),
        ],
        in_specs=[vmem] * (2 + len(blocks)),
        out_specs=[vmem] * 2,
        compiler_params=pltpu.CompilerParams(vmem_limit_bytes=VMEM_LIMIT),
        name="far_before",
    )(own, part, *blocks)


def far_after(own, part, blocks):
    vmem = pl.BlockSpec(memory_space=pltpu.VMEM)
    pairs = (len(blocks) + 1) * own.shape[1] ** 2
    return pl.pallas_call(
        after_kernel,
        out_shape=jax.ShapeDtypeStruct(own.shape, F32),
        in_specs=[vmem] * (2 + len(blocks)),
        out_specs=vmem,
        compiler_params=pltpu.CompilerParams(vmem_limit_bytes=VMEM_LIMIT),
        cost_estimate=pl.CostEstimate(flops=PAIR_FLOPS * pairs, bytes_accessed=0, transcendentals=pairs),
        name="far_after",
    )(own, part, *blocks)


def flips(size, bit):
    return [(i, i ^ bit) for i in range(size)]


ORDER = (2, 3, 1)
LATER = (4, 8, 16, 32)


def shards(positions, density, upsample, cell_map, near_list):
    columns = lax.axis_size("blk")
    peers = lax.axis_size("nbr")
    own = jnp.concatenate([positions, density, jnp.zeros((2, positions.shape[1]), F32)], axis=0)
    own, part = far_first(own)
    zs = [lax.ppermute(own, "blk", flips(columns, b)) for b in ORDER]
    tiles = near_panels(own, jnp.swapaxes(near_list, 1, 2), cell_map, upsample.shape[0], peers)
    near = [lax.ppermute(t, "nbr", flips(peers, d + 1)) for d, t in enumerate(tiles)]
    held, part = far_before(own, part, zs)
    last = None
    for bit in LATER:
        if bit >= columns:
            break
        got = lax.ppermute(held, "blk", flips(columns, bit))
        if last is None:
            part = far_after(own, part, zs)
            part = pair_sums("near", own, part, [], near, upsample)
        else:
            part = pair_sums("far_%d" % bit, own, part, [last], [], upsample)
        held = jnp.concatenate([held, got])
        last = got
    return pair_sums("far_last", own, part, [last], [], upsample, final=True)


def solution(mesh):
    placed = (
        P(None, ("blk", "nbr")),
        P(None, ("blk", "nbr")),
        P(),
        P("blk", None),
        P(("blk", "nbr"), None, None),
    )
    return jax.shard_map(
        shards, mesh=mesh, in_specs=placed, out_specs=P(None, ("blk", "nbr")), check_vma=False
    )
```

```python
import functools
import math

import jax
import jax.numpy as jnp
from jax import lax
from jax.experimental import pallas as pl
from jax.experimental.pallas import tpu as pltpu
from jax.sharding import PartitionSpec as P

FAR_REG_SQ = 0.0625
NEAR_REG_SQ = 0.01
STOKES_COEF = 1.0 / (8.0 * math.pi)
F32 = jnp.float32
BF16 = jnp.bfloat16
LANES = 128
ROWS = 8
VMEM_LIMIT = 40 * 2**20
WIDE = 2048
USED = 6
FIRST = 1
AHEAD = 1
SOON = 2
PACK_FLOPS = 900 * 10**6
PAIR_FLOPS = 3500


def split3(a):
    hi = a.astype(BF16).astype(F32)
    rest = a - hi
    mid = rest.astype(BF16).astype(F32)
    return hi, mid, rest - mid


def split2(a):
    hi = a.astype(BF16)
    return hi, (a - hi.astype(F32)).astype(BF16)


def stack_left(a):
    hi, mid, lo = split3(a)
    return jnp.concatenate([hi, hi, mid, mid, hi, lo], axis=0).astype(BF16)


def stack_right(a):
    hi, mid, lo = split3(a)
    return jnp.concatenate([hi, mid, hi, mid, lo, hi], axis=0).astype(BF16)


def stack_two(a):
    hi = a.astype(BF16).astype(F32)
    return jnp.concatenate([hi, a - hi], axis=0).astype(BF16)


def pad_rows(parts):
    have = sum(p.shape[0] for p in parts)
    return jnp.concatenate(parts + [jnp.zeros((ROWS - have, parts[0].shape[1]), F32)], axis=0)


def dot_first(a, b):
    return lax.dot_general(a, b, (((0,), (0,)), ((), ())), preferred_element_type=F32)


def dot(a, b):
    return jnp.dot(a, b, preferred_element_type=F32)


def target_features(x, reg_sq):
    inv = 1.0 / reg_sq
    ones = jnp.ones((1, x.shape[1]), F32)
    norm = jnp.sum(x * x, axis=0, keepdims=True) * inv
    dist = stack_right(pad_rows([(-2.0 * inv) * x, ones, norm]))
    return dist


def project_features(x):
    return stack_right(pad_rows([x, jnp.ones((1, x.shape[1]), F32)]))


def block_sum(source, dist_t, proj_t, reg_sq):
    inv = 1.0 / reg_sq
    inv_len = 1.0 / math.sqrt(reg_sq)
    y = source[0:3]
    f = source[3:6]
    ones = jnp.ones((1, y.shape[1]), F32)
    norm = jnp.sum(y * y, axis=0, keepdims=True) * inv + 1.0
    along = jnp.sum(y * f, axis=0, keepdims=True)
    dist_s = stack_left(pad_rows([y, norm, ones]))
    proj_s = stack_left(pad_rows([f, -along]))
    first = stack_two(pad_rows([f * inv_len]))
    second = stack_two(pad_rows([-y, ones]) * inv_len**3)
    root = lax.rsqrt(dot_first(dist_s, dist_t))
    cube = root * root * root
    lead_hi, lead_lo = split2(root + cube)
    q_hi, q_lo = split2(dot_first(proj_s, proj_t) * cube)
    return (dot(first, lead_hi) + dot(first, lead_lo)) + (dot(second, q_hi) + dot(second, q_lo))


def upsample_tiles(tiles, table):
    panel_pts, fine_pts = table.shape
    group = LANES // panel_pts
    zero = jnp.zeros((panel_pts, fine_pts), F32)
    spread = jnp.concatenate(
        [jnp.concatenate([table if h == g else zero for h in range(group)], axis=1) for g in range(group)], axis=0
    )
    t_hi, t_mid, t_lo = split3(jnp.concatenate(tiles, axis=0))
    w_hi, w_mid, w_lo = (w.astype(BF16) for w in split3(spread))
    n = t_hi.shape[0]
    on_hi = dot(jnp.concatenate([t_hi, t_mid, t_lo], axis=0).astype(BF16), w_hi)
    on_mid = dot(jnp.concatenate([t_hi, t_mid], axis=0).astype(BF16), w_mid)
    on_lo = dot(t_hi.astype(BF16), w_lo)
    fine = on_hi[0:n] + (on_hi[n : 2 * n] + on_mid[0:n]) + (on_hi[2 * n :] + on_mid[n:] + on_lo)
    ratio = panel_pts / fine_pts
    scale = jnp.where(lax.broadcasted_iota(jnp.int32, fine.shape, 0) % ROWS < 3, 1.0, ratio)
    fine = fine * scale
    return [fine[ROWS * i : ROWS * (i + 1)] for i in range(len(tiles))]


def pick_panels(peers, slots, panel_pts, own_ref, list_ref, map_ref, *rest):
    *tile_refs, table, count = rest
    entries = list_ref.shape[2]
    me = lax.axis_index("nbr")
    for i in range(peers * slots + 1):
        table[i] = -1
    for i in range(peers + 1):
        count[i] = 0

    def place(e, _):
        panel = list_ref[0, 0, e]
        cell = list_ref[0, 1, e]
        valid = cell >= 0
        dest = map_ref[0, jnp.maximum(cell, 0)]
        at = jnp.where(valid, dest, peers)
        rank = count[at]
        count[at] = rank + 1
        table[jnp.where(valid, dest * slots + rank, peers * slots)] = panel
        return 0

    lax.fori_loop(0, entries, place, 0, unroll=entries <= 16)
    group = LANES // panel_pts
    lane_group = lax.broadcasted_iota(jnp.int32, (ROWS, LANES), 1) // panel_pts
    for d in range(1, peers):
        dest = me ^ d
        tile = jnp.zeros((ROWS, LANES), F32)
        for s in range(slots):
            panel = table[dest * slots + s]
            safe = jnp.maximum(panel, 0)
            start = pl.multiple_of((safe // group) * LANES, LANES)
            piece = own_ref[:, pl.ds(start, LANES)]
            shift = (s - safe % group + group) % group * panel_pts
            moved = pltpu.roll(piece, shift, 1)
            tile = jnp.where((lane_group == s) & (panel >= 0), moved, tile)
        tile_refs[d - 1][0] = tile


def near_panels(own, near_list, cell_map, panel_pts, peers):
    slots = LANES // panel_pts
    vmem = pl.BlockSpec(memory_space=pltpu.VMEM)
    smem = pl.BlockSpec(memory_space=pltpu.SMEM)
    tile = jax.ShapeDtypeStruct((1, ROWS, LANES), F32)
    return pl.pallas_call(
        functools.partial(pick_panels, peers, slots, panel_pts),
        out_shape=[tile] * (peers - 1),
        in_specs=[vmem, smem, smem],
        out_specs=[vmem] * (peers - 1),
        scratch_shapes=[pltpu.SMEM((peers * slots + 1,), jnp.int32), pltpu.SMEM((peers + 1,), jnp.int32)],
        compiler_params=pltpu.CompilerParams(vmem_limit_bytes=VMEM_LIMIT),
        cost_estimate=pl.CostEstimate(flops=PACK_FLOPS, bytes_accessed=0, transcendentals=0),
        name="panels",
    )(own, near_list, cell_map)


def wide_blocks(refs):
    singles = []
    for ref in refs:
        if ref.shape[0] <= ROWS:
            singles.append(ref[0:USED, :])
        else:
            singles += [ref[USED * i : USED * (i + 1), :] for i in range(ref.shape[0] // USED)]
    group = max(1, WIDE // singles[0].shape[1])
    return [jnp.concatenate(singles[i : i + group], axis=1) for i in range(0, len(singles), group)]


def sum_kernel(n_far, n_near, has_prior, final, *refs):
    refs = list(refs)
    x_ref = refs.pop(0)
    prior = refs.pop(0)[...] if has_prior else None
    far_refs = [refs.pop(0) for _ in range(n_far)]
    near_refs = [refs.pop(0) for _ in range(n_near)]
    table_ref = refs.pop(0) if n_near else None
    out_ref = refs.pop(0)
    x = x_ref[0:3, :]
    proj_t = project_features(x)
    total = jnp.zeros((2 * ROWS, x.shape[1]), F32)
    if n_far:
        dist_t = target_features(x, FAR_REG_SQ)
        for block in wide_blocks(far_refs):
            total = total + block_sum(block, dist_t, proj_t, FAR_REG_SQ)
    if n_near:
        dist_t = target_features(x, NEAR_REG_SQ)
        tiles = []
        for ref in near_refs:
            tiles += [ref[i] for i in range(ref.shape[0])]
        for start in range(0, len(tiles), 3):
            fine = upsample_tiles(tiles[start : start + 3], table_ref[...])
            total = total + block_sum(jnp.concatenate(fine, axis=1), dist_t, proj_t, NEAR_REG_SQ)
    summed = total[0:ROWS] + total[ROWS:]
    if has_prior:
        summed = summed + prior
    if final:
        out_ref[...] = STOKES_COEF * (summed[0:3] + x * summed[3:4])
    else:
        out_ref[...] = summed


def pair_sums(name, own, prior, far, near, table, final=False):
    points = own.shape[1]
    vmem = pl.BlockSpec(memory_space=pltpu.VMEM)
    args = [own] + ([prior] if prior is not None else []) + list(far) + list(near) + ([table] if near else [])
    far_sources = sum(a.size // ROWS for a in far)
    near_sources = sum(a.size // ROWS for a in near) * table.shape[1] // table.shape[0]
    pairs = points * (far_sources + near_sources)
    out_shape = [jax.ShapeDtypeStruct((3 if final else ROWS, points), F32)]
    got = pl.pallas_call(
        functools.partial(sum_kernel, len(far), len(near), prior is not None, final),
        out_shape=out_shape,
        in_specs=[vmem] * len(args),
        out_specs=[vmem] * len(out_shape),
        compiler_params=pltpu.CompilerParams(vmem_limit_bytes=VMEM_LIMIT),
        cost_estimate=pl.CostEstimate(flops=PAIR_FLOPS * pairs, bytes_accessed=0, transcendentals=pairs),
        name=name,
    )(*args)
    return got[0]


def place():
    blk = lax.axis_index("blk")
    first = jnp.logical_and(blk < FIRST, lax.axis_index("nbr") < lax.axis_size("nbr") // 2)
    soon = jnp.logical_and(jnp.logical_not(first), blk < SOON * (lax.axis_size("blk") // 4))
    late = jnp.logical_not(jnp.logical_or(first, soon))
    return first, soon, late


def far_total(x, blocks, part=None):
    total = jnp.zeros((2 * ROWS, x.shape[1]), F32)
    dist_t = target_features(x, FAR_REG_SQ)
    proj_t = project_features(x)
    for block in wide_blocks(blocks):
        total = total + block_sum(block, dist_t, proj_t, FAR_REG_SQ)
    total = total[0:ROWS] + total[ROWS:]
    return total if part is None else part + total


def first_kernel(own_ref, copy_ref, out_ref):
    first, soon, late = place()
    copy_ref[0:USED, :] = own_ref[...]
    copy_ref[USED:, :] = jnp.zeros((ROWS - USED, own_ref.shape[1]), F32)

    @pl.when(first)
    def _():
        out_ref[...] = far_total(own_ref[0:3, :], [own_ref])

    @pl.when(jnp.logical_not(first))
    def _():
        out_ref[...] = jnp.zeros(out_ref.shape, F32)


def before_kernel(own_ref, part_ref, *refs):
    *block_refs, held_ref, out_ref = refs
    first, soon, late = place()
    for i, ref in enumerate([own_ref, *block_refs]):
        held_ref[USED * i : USED * (i + 1), :] = ref[0:USED, :]

    @pl.when(first)
    def _():
        out_ref[...] = far_total(own_ref[0:3, :], block_refs[:AHEAD], part_ref[...])

    @pl.when(soon)
    def _():
        out_ref[...] = far_total(own_ref[0:3, :], [own_ref], part_ref[...])

    @pl.when(late)
    def _():
        out_ref[...] = part_ref[...]


def after_kernel(own_ref, part_ref, *refs):
    *block_refs, out_ref = refs
    first, soon, late = place()

    @pl.when(first)
    def _():
        out_ref[...] = far_total(own_ref[0:3, :], block_refs[AHEAD:], part_ref[...])

    @pl.when(soon)
    def _():
        out_ref[...] = far_total(own_ref[0:3, :], block_refs, part_ref[...])

    @pl.when(late)
    def _():
        out_ref[...] = far_total(own_ref[0:3, :], [own_ref, *block_refs], part_ref[...])


def far_first(own):
    vmem = pl.BlockSpec(memory_space=pltpu.VMEM)
    return pl.pallas_call(
        first_kernel,
        out_shape=[jax.ShapeDtypeStruct((ROWS, own.shape[1]), F32)] * 2,
        in_specs=[vmem],
        out_specs=[vmem] * 2,
        compiler_params=pltpu.CompilerParams(vmem_limit_bytes=VMEM_LIMIT),
        name="far_first",
    )(own)


def far_before(own, part, blocks):
    vmem = pl.BlockSpec(memory_space=pltpu.VMEM)
    return pl.pallas_call(
        before_kernel,
        out_shape=[
            jax.ShapeDtypeStruct((USED * (len(blocks) + 1), own.shape[1]), F32),
            jax.ShapeDtypeStruct(own.shape, F32),
        ],
        in_specs=[vmem] * (2 + len(blocks)),
        out_specs=[vmem] * 2,
        compiler_params=pltpu.CompilerParams(vmem_limit_bytes=VMEM_LIMIT),
        name="far_before",
    )(own, part, *blocks)


def far_after(own, part, blocks):
    vmem = pl.BlockSpec(memory_space=pltpu.VMEM)
    pairs = (len(blocks) + 1) * own.shape[1] ** 2
    return pl.pallas_call(
        after_kernel,
        out_shape=jax.ShapeDtypeStruct(own.shape, F32),
        in_specs=[vmem] * (2 + len(blocks)),
        out_specs=vmem,
        compiler_params=pltpu.CompilerParams(vmem_limit_bytes=VMEM_LIMIT),
        cost_estimate=pl.CostEstimate(flops=PAIR_FLOPS * pairs, bytes_accessed=0, transcendentals=pairs),
        name="far_after",
    )(own, part, *blocks)


def flips(size, bit):
    return [(i, i ^ bit) for i in range(size)]


ORDER = (2, 3, 1)
LATER = (4, 8, 16, 32)


def shards(positions, density, upsample, cell_map, near_list):
    columns = lax.axis_size("blk")
    peers = lax.axis_size("nbr")
    own = jnp.concatenate([positions, density], axis=0)
    own, part = far_first(own)
    zs = [lax.ppermute(own, "blk", flips(columns, b)) for b in ORDER]
    tiles = near_panels(own, jnp.swapaxes(near_list, 1, 2), cell_map, upsample.shape[0], peers)
    near = [lax.ppermute(t, "nbr", flips(peers, d + 1)) for d, t in enumerate(tiles)]
    held, part = far_before(own, part, zs)
    last = None
    for bit in LATER:
        if bit >= columns:
            break
        got = lax.ppermute(held, "blk", flips(columns, bit))
        if last is None:
            part = far_after(own, part, zs)
            part = pair_sums("near", own, part, [], near, upsample)
        else:
            part = pair_sums("far_%d" % bit, own, part, [last], [], upsample)
        held = jnp.concatenate([held, got])
        last = got
    return pair_sums("far_last", own, part, [last], [], upsample, final=True)


def solution(mesh):
    placed = (
        P(None, ("blk", "nbr")),
        P(None, ("blk", "nbr")),
        P(),
        P("blk", None),
        P(("blk", "nbr"), None, None),
    )
    return jax.shard_map(
        shards, mesh=mesh, in_specs=placed, out_specs=P(None, ("blk", "nbr")), check_vma=False
    )
```

```python
import functools
import math

import jax
import jax.numpy as jnp
from jax import lax
from jax.experimental import pallas as pl
from jax.experimental.pallas import tpu as pltpu
from jax.sharding import PartitionSpec as P

FAR_REG_SQ = 0.0625
NEAR_REG_SQ = 0.01
STOKES_COEF = 1.0 / (8.0 * math.pi)
F32 = jnp.float32
BF16 = jnp.bfloat16
LANES = 128
ROWS = 8
VMEM_LIMIT = 40 * 2**20
WIDE = 2048
USED = 6
FIRST = 1
SOON = 2
PACK_FLOPS = 900 * 10**6
PAIR_FLOPS = 3500


def split3(a):
    hi = a.astype(BF16).astype(F32)
    rest = a - hi
    mid = rest.astype(BF16).astype(F32)
    return hi, mid, rest - mid


def split2(a):
    hi = a.astype(BF16)
    return hi, (a - hi.astype(F32)).astype(BF16)


def stack_left(a):
    hi, mid, lo = split3(a)
    return jnp.concatenate([hi, hi, mid, mid, hi, lo], axis=0).astype(BF16)


def stack_right(a):
    hi, mid, lo = split3(a)
    return jnp.concatenate([hi, mid, hi, mid, lo, hi], axis=0).astype(BF16)


def stack_two(a):
    hi = a.astype(BF16).astype(F32)
    return jnp.concatenate([hi, a - hi], axis=0).astype(BF16)


def pad_rows(parts):
    have = sum(p.shape[0] for p in parts)
    return jnp.concatenate(parts + [jnp.zeros((ROWS - have, parts[0].shape[1]), F32)], axis=0)


def dot_first(a, b):
    return lax.dot_general(a, b, (((0,), (0,)), ((), ())), preferred_element_type=F32)


def dot(a, b):
    return jnp.dot(a, b, preferred_element_type=F32)


def target_features(x, reg_sq):
    inv = 1.0 / reg_sq
    ones = jnp.ones((1, x.shape[1]), F32)
    norm = jnp.sum(x * x, axis=0, keepdims=True) * inv
    dist = stack_right(pad_rows([(-2.0 * inv) * x, ones, norm]))
    return dist


def project_features(x):
    return stack_right(pad_rows([x, jnp.ones((1, x.shape[1]), F32)]))


def block_sum(source, dist_t, proj_t, reg_sq):
    inv = 1.0 / reg_sq
    inv_len = 1.0 / math.sqrt(reg_sq)
    y = source[0:3]
    f = source[3:6]
    ones = jnp.ones((1, y.shape[1]), F32)
    norm = jnp.sum(y * y, axis=0, keepdims=True) * inv + 1.0
    along = jnp.sum(y * f, axis=0, keepdims=True)
    dist_s = stack_left(pad_rows([y, norm, ones]))
    proj_s = stack_left(pad_rows([f, -along]))
    first = stack_two(pad_rows([f * inv_len]))
    second = stack_two(pad_rows([-y, ones]) * inv_len**3)
    root = lax.rsqrt(dot_first(dist_s, dist_t))
    cube = root * root * root
    lead_hi, lead_lo = split2(root + cube)
    q_hi, q_lo = split2(dot_first(proj_s, proj_t) * cube)
    return (dot(first, lead_hi) + dot(first, lead_lo)) + (dot(second, q_hi) + dot(second, q_lo))


def upsample_tiles(tiles, table):
    panel_pts, fine_pts = table.shape
    group = LANES // panel_pts
    zero = jnp.zeros((panel_pts, fine_pts), F32)
    spread = jnp.concatenate(
        [jnp.concatenate([table if h == g else zero for h in range(group)], axis=1) for g in range(group)], axis=0
    )
    t_hi, t_mid, t_lo = split3(jnp.concatenate(tiles, axis=0))
    w_hi, w_mid, w_lo = (w.astype(BF16) for w in split3(spread))
    n = t_hi.shape[0]
    on_hi = dot(jnp.concatenate([t_hi, t_mid, t_lo], axis=0).astype(BF16), w_hi)
    on_mid = dot(jnp.concatenate([t_hi, t_mid], axis=0).astype(BF16), w_mid)
    on_lo = dot(t_hi.astype(BF16), w_lo)
    fine = on_hi[0:n] + (on_hi[n : 2 * n] + on_mid[0:n]) + (on_hi[2 * n :] + on_mid[n:] + on_lo)
    ratio = panel_pts / fine_pts
    scale = jnp.where(lax.broadcasted_iota(jnp.int32, fine.shape, 0) % ROWS < 3, 1.0, ratio)
    fine = fine * scale
    return [fine[ROWS * i : ROWS * (i + 1)] for i in range(len(tiles))]


def pick_panels(peers, slots, panel_pts, own_ref, list_ref, map_ref, *rest):
    *tile_refs, table, count = rest
    entries = list_ref.shape[2]
    me = lax.axis_index("nbr")
    for i in range(peers * slots + 1):
        table[i] = -1
    for i in range(peers + 1):
        count[i] = 0

    def place(e, _):
        panel = list_ref[0, 0, e]
        cell = list_ref[0, 1, e]
        valid = cell >= 0
        dest = map_ref[0, jnp.maximum(cell, 0)]
        at = jnp.where(valid, dest, peers)
        rank = count[at]
        count[at] = rank + 1
        table[jnp.where(valid, dest * slots + rank, peers * slots)] = panel
        return 0

    lax.fori_loop(0, entries, place, 0, unroll=entries <= 16)
    group = LANES // panel_pts
    lane_group = lax.broadcasted_iota(jnp.int32, (ROWS, LANES), 1) // panel_pts
    for d in range(1, peers):
        dest = me ^ d
        tile = jnp.zeros((ROWS, LANES), F32)
        for s in range(slots):
            panel = table[dest * slots + s]
            safe = jnp.maximum(panel, 0)
            start = pl.multiple_of((safe // group) * LANES, LANES)
            piece = own_ref[:, pl.ds(start, LANES)]
            shift = (s - safe % group + group) % group * panel_pts
            moved = pltpu.roll(piece, shift, 1)
            tile = jnp.where((lane_group == s) & (panel >= 0), moved, tile)
        tile_refs[d - 1][0] = tile


def near_panels(own, near_list, cell_map, panel_pts, peers):
    slots = LANES // panel_pts
    vmem = pl.BlockSpec(memory_space=pltpu.VMEM)
    smem = pl.BlockSpec(memory_space=pltpu.SMEM)
    tile = jax.ShapeDtypeStruct((1, ROWS, LANES), F32)
    return pl.pallas_call(
        functools.partial(pick_panels, peers, slots, panel_pts),
        out_shape=[tile] * (peers - 1),
        in_specs=[vmem, smem, smem],
        out_specs=[vmem] * (peers - 1),
        scratch_shapes=[pltpu.SMEM((peers * slots + 1,), jnp.int32), pltpu.SMEM((peers + 1,), jnp.int32)],
        compiler_params=pltpu.CompilerParams(vmem_limit_bytes=VMEM_LIMIT),
        cost_estimate=pl.CostEstimate(flops=PACK_FLOPS, bytes_accessed=0, transcendentals=0),
        name="panels",
    )(own, near_list, cell_map)


def wide_blocks(refs):
    singles = []
    for ref in refs:
        if ref.shape[0] <= ROWS:
            singles.append(ref[0:USED, :])
        else:
            singles += [ref[USED * i : USED * (i + 1), :] for i in range(ref.shape[0] // USED)]
    group = max(1, WIDE // singles[0].shape[1])
    return [jnp.concatenate(singles[i : i + group], axis=1) for i in range(0, len(singles), group)]


def sum_kernel(n_far, n_near, has_prior, final, *refs):
    refs = list(refs)
    x_ref = refs.pop(0)
    prior = refs.pop(0)[...] if has_prior else None
    far_refs = [refs.pop(0) for _ in range(n_far)]
    near_refs = [refs.pop(0) for _ in range(n_near)]
    table_ref = refs.pop(0) if n_near else None
    out_ref = refs.pop(0)
    x = x_ref[0:3, :]
    proj_t = project_features(x)
    total = jnp.zeros((2 * ROWS, x.shape[1]), F32)
    if n_far:
        dist_t = target_features(x, FAR_REG_SQ)
        for block in wide_blocks(far_refs):
            total = total + block_sum(block, dist_t, proj_t, FAR_REG_SQ)
    if n_near:
        dist_t = target_features(x, NEAR_REG_SQ)
        tiles = []
        for ref in near_refs:
            tiles += [ref[i] for i in range(ref.shape[0])]
        for start in range(0, len(tiles), 3):
            fine = upsample_tiles(tiles[start : start + 3], table_ref[...])
            total = total + block_sum(jnp.concatenate(fine, axis=1), dist_t, proj_t, NEAR_REG_SQ)
    summed = total[0:ROWS] + total[ROWS:]
    if has_prior:
        summed = summed + prior
    if final:
        out_ref[...] = STOKES_COEF * (summed[0:3] + x * summed[3:4])
    else:
        out_ref[...] = summed


def pair_sums(name, own, prior, far, near, table, final=False):
    points = own.shape[1]
    vmem = pl.BlockSpec(memory_space=pltpu.VMEM)
    args = [own] + ([prior] if prior is not None else []) + list(far) + list(near) + ([table] if near else [])
    far_sources = sum(a.size // ROWS for a in far)
    near_sources = sum(a.size // ROWS for a in near) * table.shape[1] // table.shape[0]
    pairs = points * (far_sources + near_sources)
    out_shape = [jax.ShapeDtypeStruct((3 if final else ROWS, points), F32)]
    got = pl.pallas_call(
        functools.partial(sum_kernel, len(far), len(near), prior is not None, final),
        out_shape=out_shape,
        in_specs=[vmem] * len(args),
        out_specs=[vmem] * len(out_shape),
        compiler_params=pltpu.CompilerParams(vmem_limit_bytes=VMEM_LIMIT),
        cost_estimate=pl.CostEstimate(flops=PAIR_FLOPS * pairs, bytes_accessed=0, transcendentals=pairs),
        name=name,
    )(*args)
    return got[0]


NEEDS = 2


def ahead_of(blocks):
    half = blocks[1].shape[1] // 4
    return [blocks[0], blocks[1].at[:, 0:half]]


def rest_of(blocks):
    half = blocks[1].shape[1] // 4
    return [blocks[1].at[:, half:], *blocks[2:]]


def place():
    blk = lax.axis_index("blk")
    first = jnp.logical_and(blk < FIRST, lax.axis_index("nbr") < lax.axis_size("nbr") // 2)
    soon = jnp.logical_and(jnp.logical_not(first), blk < SOON * (lax.axis_size("blk") // 4))
    late = jnp.logical_not(jnp.logical_or(first, soon))
    return first, soon, late


def far_total(x, blocks, part=None):
    total = jnp.zeros((2 * ROWS, x.shape[1]), F32)
    dist_t = target_features(x, FAR_REG_SQ)
    proj_t = project_features(x)
    for block in wide_blocks(blocks):
        total = total + block_sum(block, dist_t, proj_t, FAR_REG_SQ)
    total = total[0:ROWS] + total[ROWS:]
    return total if part is None else part + total


def first_kernel(own_ref, copy_ref, out_ref):
    first, soon, late = place()
    copy_ref[0:USED, :] = own_ref[...]
    copy_ref[USED:, :] = jnp.zeros((ROWS - USED, own_ref.shape[1]), F32)

    @pl.when(first)
    def _():
        out_ref[...] = far_total(own_ref[0:3, :], [own_ref])

    @pl.when(jnp.logical_not(first))
    def _():
        out_ref[...] = jnp.zeros(out_ref.shape, F32)


def ahead_kernel(own_ref, part_ref, *refs):
    *block_refs, out_ref = refs
    first, soon, late = place()

    @pl.when(first)
    def _():
        out_ref[...] = far_total(own_ref[0:3, :], ahead_of(block_refs), part_ref[...])

    @pl.when(soon)
    def _():
        out_ref[...] = far_total(own_ref[0:3, :], [own_ref], part_ref[...])

    @pl.when(late)
    def _():
        out_ref[...] = part_ref[...]


def stack_kernel(own_ref, after_ref, *refs):
    *block_refs, held_ref = refs
    for i, ref in enumerate([own_ref, *block_refs]):
        held_ref[USED * i : USED * (i + 1), :] = ref[0:USED, :]


def after_kernel(own_ref, part_ref, *refs):
    *block_refs, out_ref = refs
    first, soon, late = place()

    @pl.when(first)
    def _():
        out_ref[...] = far_total(own_ref[0:3, :], rest_of(block_refs), part_ref[...])

    @pl.when(soon)
    def _():
        out_ref[...] = far_total(own_ref[0:3, :], block_refs, part_ref[...])

    @pl.when(late)
    def _():
        out_ref[...] = far_total(own_ref[0:3, :], [own_ref, *block_refs], part_ref[...])


def far_first(own):
    vmem = pl.BlockSpec(memory_space=pltpu.VMEM)
    return pl.pallas_call(
        first_kernel,
        out_shape=[jax.ShapeDtypeStruct((ROWS, own.shape[1]), F32)] * 2,
        in_specs=[vmem],
        out_specs=[vmem] * 2,
        compiler_params=pltpu.CompilerParams(vmem_limit_bytes=VMEM_LIMIT),
        name="far_first",
    )(own)


def far_ahead(own, part, blocks):
    vmem = pl.BlockSpec(memory_space=pltpu.VMEM)
    pairs = own.shape[1] ** 2
    return pl.pallas_call(
        ahead_kernel,
        out_shape=jax.ShapeDtypeStruct(own.shape, F32),
        in_specs=[vmem] * (2 + len(blocks)),
        out_specs=vmem,
        compiler_params=pltpu.CompilerParams(vmem_limit_bytes=VMEM_LIMIT),
        cost_estimate=pl.CostEstimate(flops=PAIR_FLOPS * pairs, bytes_accessed=0, transcendentals=pairs),
        name="far_ahead",
    )(own, part, *blocks)


def stack(own, after, blocks):
    vmem = pl.BlockSpec(memory_space=pltpu.VMEM)
    return pl.pallas_call(
        stack_kernel,
        out_shape=jax.ShapeDtypeStruct((USED * (len(blocks) + 1), own.shape[1]), F32),
        in_specs=[vmem, pl.BlockSpec(memory_space=pl.ANY)] + [vmem] * len(blocks),
        out_specs=vmem,
        compiler_params=pltpu.CompilerParams(vmem_limit_bytes=VMEM_LIMIT),
        name="stack",
    )(own, after, *blocks)


def far_after(own, part, blocks):
    vmem = pl.BlockSpec(memory_space=pltpu.VMEM)
    pairs = (len(blocks) + 1) * own.shape[1] ** 2
    return pl.pallas_call(
        after_kernel,
        out_shape=jax.ShapeDtypeStruct(own.shape, F32),
        in_specs=[vmem] * (2 + len(blocks)),
        out_specs=vmem,
        compiler_params=pltpu.CompilerParams(vmem_limit_bytes=VMEM_LIMIT),
        cost_estimate=pl.CostEstimate(flops=PAIR_FLOPS * pairs, bytes_accessed=0, transcendentals=pairs),
        name="far_after",
    )(own, part, *blocks)


def flips(size, bit):
    return [(i, i ^ bit) for i in range(size)]


ORDER = (2, 3, 1)
LATER = (4, 8, 16, 32)


def shards(positions, density, upsample, cell_map, near_list):
    columns = lax.axis_size("blk")
    peers = lax.axis_size("nbr")
    own = jnp.concatenate([positions, density], axis=0)
    own, part = far_first(own)
    zs = [lax.ppermute(own, "blk", flips(columns, b)) for b in ORDER]
    tiles = near_panels(own, jnp.swapaxes(near_list, 1, 2), cell_map, upsample.shape[0], peers)
    near = [lax.ppermute(t, "nbr", flips(peers, d + 1)) for d, t in enumerate(tiles)]
    part = far_ahead(own, part, zs[:NEEDS])
    held = stack(own, part, zs)
    last = None
    for bit in LATER:
        if bit >= columns:
            break
        got = lax.ppermute(held, "blk", flips(columns, bit))
        if last is None:
            part = far_after(own, part, zs)
            part = pair_sums("near", own, part, [], near, upsample)
        else:
            part = pair_sums("far_%d" % bit, own, part, [last], [], upsample)
        held = jnp.concatenate([held, got])
        last = got
    return pair_sums("far_last", own, part, [last], [], upsample, final=True)


def solution(mesh):
    placed = (
        P(None, ("blk", "nbr")),
        P(None, ("blk", "nbr")),
        P(),
        P("blk", None),
        P(("blk", "nbr"), None, None),
    )
    return jax.shard_map(
        shards, mesh=mesh, in_specs=placed, out_specs=P(None, ("blk", "nbr")), check_vma=False
    )
```

```python
import functools
import math

import jax
import jax.numpy as jnp
from jax import lax
from jax.experimental import pallas as pl
from jax.experimental.pallas import tpu as pltpu
from jax.sharding import PartitionSpec as P

FAR_REG_SQ = 0.0625
NEAR_REG_SQ = 0.01
STOKES_COEF = 1.0 / (8.0 * math.pi)
F32 = jnp.float32
BF16 = jnp.bfloat16
LANES = 128
ROWS = 8
VMEM_LIMIT = 40 * 2**20
WIDE = 2048
USED = 6
FIRST = 1
SOON = 1
PACK_FLOPS = 900 * 10**6
PAIR_FLOPS = 3500


def split3(a):
    hi = a.astype(BF16).astype(F32)
    rest = a - hi
    mid = rest.astype(BF16).astype(F32)
    return hi, mid, rest - mid


def split2(a):
    hi = a.astype(BF16)
    return hi, (a - hi.astype(F32)).astype(BF16)


def stack_left(a):
    hi, mid, lo = split3(a)
    return jnp.concatenate([hi, hi, mid, mid, hi, lo], axis=0).astype(BF16)


def stack_right(a):
    hi, mid, lo = split3(a)
    return jnp.concatenate([hi, mid, hi, mid, lo, hi], axis=0).astype(BF16)


def stack_two(a):
    hi = a.astype(BF16).astype(F32)
    return jnp.concatenate([hi, a - hi], axis=0).astype(BF16)


def pad_rows(parts):
    have = sum(p.shape[0] for p in parts)
    return jnp.concatenate(parts + [jnp.zeros((ROWS - have, parts[0].shape[1]), F32)], axis=0)


def dot_first(a, b):
    return lax.dot_general(a, b, (((0,), (0,)), ((), ())), preferred_element_type=F32)


def dot(a, b):
    return jnp.dot(a, b, preferred_element_type=F32)


def target_features(x, reg_sq):
    inv = 1.0 / reg_sq
    ones = jnp.ones((1, x.shape[1]), F32)
    norm = jnp.sum(x * x, axis=0, keepdims=True) * inv
    dist = stack_right(pad_rows([(-2.0 * inv) * x, ones, norm]))
    return dist


def project_features(x):
    return stack_right(pad_rows([x, jnp.ones((1, x.shape[1]), F32)]))


def block_sum(source, dist_t, proj_t, reg_sq):
    inv = 1.0 / reg_sq
    inv_len = 1.0 / math.sqrt(reg_sq)
    y = source[0:3]
    f = source[3:6]
    ones = jnp.ones((1, y.shape[1]), F32)
    norm = jnp.sum(y * y, axis=0, keepdims=True) * inv + 1.0
    along = jnp.sum(y * f, axis=0, keepdims=True)
    dist_s = stack_left(pad_rows([y, norm, ones]))
    proj_s = stack_left(pad_rows([f, -along]))
    first = stack_two(pad_rows([f * inv_len]))
    second = stack_two(pad_rows([-y, ones]) * inv_len**3)
    root = lax.rsqrt(dot_first(dist_s, dist_t))
    cube = root * root * root
    lead_hi, lead_lo = split2(root + cube)
    q_hi, q_lo = split2(dot_first(proj_s, proj_t) * cube)
    return (dot(first, lead_hi) + dot(first, lead_lo)) + (dot(second, q_hi) + dot(second, q_lo))


def upsample_tiles(tiles, table):
    panel_pts, fine_pts = table.shape
    group = LANES // panel_pts
    zero = jnp.zeros((panel_pts, fine_pts), F32)
    spread = jnp.concatenate(
        [jnp.concatenate([table if h == g else zero for h in range(group)], axis=1) for g in range(group)], axis=0
    )
    t_hi, t_mid, t_lo = split3(jnp.concatenate(tiles, axis=0))
    w_hi, w_mid, w_lo = (w.astype(BF16) for w in split3(spread))
    n = t_hi.shape[0]
    on_hi = dot(jnp.concatenate([t_hi, t_mid, t_lo], axis=0).astype(BF16), w_hi)
    on_mid = dot(jnp.concatenate([t_hi, t_mid], axis=0).astype(BF16), w_mid)
    on_lo = dot(t_hi.astype(BF16), w_lo)
    fine = on_hi[0:n] + (on_hi[n : 2 * n] + on_mid[0:n]) + (on_hi[2 * n :] + on_mid[n:] + on_lo)
    ratio = panel_pts / fine_pts
    scale = jnp.where(lax.broadcasted_iota(jnp.int32, fine.shape, 0) % ROWS < 3, 1.0, ratio)
    fine = fine * scale
    return [fine[ROWS * i : ROWS * (i + 1)] for i in range(len(tiles))]


def pick_panels(peers, slots, panel_pts, own_ref, list_ref, map_ref, *rest):
    *tile_refs, table, count = rest
    entries = list_ref.shape[2]
    me = lax.axis_index("nbr")
    for i in range(peers * slots + 1):
        table[i] = -1
    for i in range(peers + 1):
        count[i] = 0

    def place(e, _):
        panel = list_ref[0, 0, e]
        cell = list_ref[0, 1, e]
        valid = cell >= 0
        dest = map_ref[0, jnp.maximum(cell, 0)]
        at = jnp.where(valid, dest, peers)
        rank = count[at]
        count[at] = rank + 1
        table[jnp.where(valid, dest * slots + rank, peers * slots)] = panel
        return 0

    lax.fori_loop(0, entries, place, 0, unroll=entries <= 16)
    group = LANES // panel_pts
    lane_group = lax.broadcasted_iota(jnp.int32, (ROWS, LANES), 1) // panel_pts
    for d in range(1, peers):
        dest = me ^ d
        tile = jnp.zeros((ROWS, LANES), F32)
        for s in range(slots):
            panel = table[dest * slots + s]
            safe = jnp.maximum(panel, 0)
            start = pl.multiple_of((safe // group) * LANES, LANES)
            piece = own_ref[:, pl.ds(start, LANES)]
            shift = (s - safe % group + group) % group * panel_pts
            moved = pltpu.roll(piece, shift, 1)
            tile = jnp.where((lane_group == s) & (panel >= 0), moved, tile)
        tile_refs[d - 1][0] = tile


def near_panels(own, near_list, cell_map, panel_pts, peers):
    slots = LANES // panel_pts
    vmem = pl.BlockSpec(memory_space=pltpu.VMEM)
    smem = pl.BlockSpec(memory_space=pltpu.SMEM)
    tile = jax.ShapeDtypeStruct((1, ROWS, LANES), F32)
    return pl.pallas_call(
        functools.partial(pick_panels, peers, slots, panel_pts),
        out_shape=[tile] * (peers - 1),
        in_specs=[vmem, smem, smem],
        out_specs=[vmem] * (peers - 1),
        scratch_shapes=[pltpu.SMEM((peers * slots + 1,), jnp.int32), pltpu.SMEM((peers + 1,), jnp.int32)],
        compiler_params=pltpu.CompilerParams(vmem_limit_bytes=VMEM_LIMIT),
        cost_estimate=pl.CostEstimate(flops=PACK_FLOPS, bytes_accessed=0, transcendentals=0),
        name="panels",
    )(own, near_list, cell_map)


def wide_blocks(refs):
    singles = []
    for ref in refs:
        if ref.shape[0] <= ROWS:
            singles.append(ref[0:USED, :])
        else:
            singles += [ref[USED * i : USED * (i + 1), :] for i in range(ref.shape[0] // USED)]
    group = max(1, WIDE // singles[0].shape[1])
    return [jnp.concatenate(singles[i : i + group], axis=1) for i in range(0, len(singles), group)]


def sum_kernel(n_far, n_near, has_prior, final, *refs):
    refs = list(refs)
    x_ref = refs.pop(0)
    prior = refs.pop(0)[...] if has_prior else None
    far_refs = [refs.pop(0) for _ in range(n_far)]
    near_refs = [refs.pop(0) for _ in range(n_near)]
    table_ref = refs.pop(0) if n_near else None
    out_ref = refs.pop(0)
    x = x_ref[0:3, :]
    proj_t = project_features(x)
    total = jnp.zeros((2 * ROWS, x.shape[1]), F32)
    if n_far:
        dist_t = target_features(x, FAR_REG_SQ)
        for block in wide_blocks(far_refs):
            total = total + block_sum(block, dist_t, proj_t, FAR_REG_SQ)
    if n_near:
        dist_t = target_features(x, NEAR_REG_SQ)
        tiles = []
        for ref in near_refs:
            tiles += [ref[i] for i in range(ref.shape[0])]
        for start in range(0, len(tiles), 3):
            fine = upsample_tiles(tiles[start : start + 3], table_ref[...])
            total = total + block_sum(jnp.concatenate(fine, axis=1), dist_t, proj_t, NEAR_REG_SQ)
    summed = total[0:ROWS] + total[ROWS:]
    if has_prior:
        summed = summed + prior
    if final:
        out_ref[...] = STOKES_COEF * (summed[0:3] + x * summed[3:4])
    else:
        out_ref[...] = summed


def pair_sums(name, own, prior, far, near, table, final=False):
    points = own.shape[1]
    vmem = pl.BlockSpec(memory_space=pltpu.VMEM)
    args = [own] + ([prior] if prior is not None else []) + list(far) + list(near) + ([table] if near else [])
    far_sources = sum(a.size // ROWS for a in far)
    near_sources = sum(a.size // ROWS for a in near) * table.shape[1] // table.shape[0]
    pairs = points * (far_sources + near_sources)
    out_shape = [jax.ShapeDtypeStruct((3 if final else ROWS, points), F32)]
    got = pl.pallas_call(
        functools.partial(sum_kernel, len(far), len(near), prior is not None, final),
        out_shape=out_shape,
        in_specs=[vmem] * len(args),
        out_specs=[vmem] * len(out_shape),
        compiler_params=pltpu.CompilerParams(vmem_limit_bytes=VMEM_LIMIT),
        cost_estimate=pl.CostEstimate(flops=PAIR_FLOPS * pairs, bytes_accessed=0, transcendentals=pairs),
        name=name,
    )(*args)
    return got[0]


NEEDS = 2


def ahead_of(blocks):
    half = blocks[1].shape[1] // 4
    return [blocks[0], blocks[1].at[:, 0:half]]


def rest_of(blocks):
    half = blocks[1].shape[1] // 4
    return [blocks[1].at[:, half:], *blocks[2:]]


def place():
    blk = lax.axis_index("blk")
    first = jnp.logical_and(blk < FIRST, lax.axis_index("nbr") < lax.axis_size("nbr") // 2)
    soon = jnp.logical_and(jnp.logical_not(first), blk < SOON * (lax.axis_size("blk") // 4))
    late = jnp.logical_not(jnp.logical_or(first, soon))
    return first, soon, late


def far_total(x, blocks, part=None):
    total = jnp.zeros((2 * ROWS, x.shape[1]), F32)
    dist_t = target_features(x, FAR_REG_SQ)
    proj_t = project_features(x)
    for block in wide_blocks(blocks):
        total = total + block_sum(block, dist_t, proj_t, FAR_REG_SQ)
    total = total[0:ROWS] + total[ROWS:]
    return total if part is None else part + total


def first_kernel(own_ref, copy_ref, out_ref):
    first, soon, late = place()
    copy_ref[0:USED, :] = own_ref[...]
    copy_ref[USED:, :] = jnp.zeros((ROWS - USED, own_ref.shape[1]), F32)

    @pl.when(first)
    def _():
        out_ref[...] = far_total(own_ref[0:3, :], [own_ref])

    @pl.when(jnp.logical_not(first))
    def _():
        out_ref[...] = jnp.zeros(out_ref.shape, F32)


def ahead_kernel(own_ref, part_ref, *refs):
    *block_refs, out_ref = refs
    first, soon, late = place()

    @pl.when(first)
    def _():
        out_ref[...] = far_total(own_ref[0:3, :], ahead_of(block_refs), part_ref[...])

    @pl.when(soon)
    def _():
        out_ref[...] = far_total(own_ref[0:3, :], [own_ref], part_ref[...])

    @pl.when(late)
    def _():
        out_ref[...] = part_ref[...]


def stack_kernel(own_ref, after_ref, *refs):
    *block_refs, held_ref = refs
    for i, ref in enumerate([own_ref, *block_refs]):
        held_ref[USED * i : USED * (i + 1), :] = ref[0:USED, :]


def after_kernel(own_ref, part_ref, *refs):
    *block_refs, out_ref = refs
    first, soon, late = place()

    @pl.when(first)
    def _():
        out_ref[...] = far_total(own_ref[0:3, :], rest_of(block_refs), part_ref[...])

    @pl.when(soon)
    def _():
        out_ref[...] = far_total(own_ref[0:3, :], block_refs, part_ref[...])

    @pl.when(late)
    def _():
        out_ref[...] = far_total(own_ref[0:3, :], [own_ref, *block_refs], part_ref[...])


def far_first(own):
    vmem = pl.BlockSpec(memory_space=pltpu.VMEM)
    return pl.pallas_call(
        first_kernel,
        out_shape=[jax.ShapeDtypeStruct((ROWS, own.shape[1]), F32)] * 2,
        in_specs=[vmem],
        out_specs=[vmem] * 2,
        compiler_params=pltpu.CompilerParams(vmem_limit_bytes=VMEM_LIMIT),
        name="far_first",
    )(own)


def far_ahead(own, part, blocks):
    vmem = pl.BlockSpec(memory_space=pltpu.VMEM)
    pairs = own.shape[1] ** 2
    return pl.pallas_call(
        ahead_kernel,
        out_shape=jax.ShapeDtypeStruct(own.shape, F32),
        in_specs=[vmem] * (2 + len(blocks)),
        out_specs=vmem,
        compiler_params=pltpu.CompilerParams(vmem_limit_bytes=VMEM_LIMIT),
        cost_estimate=pl.CostEstimate(flops=PAIR_FLOPS * pairs, bytes_accessed=0, transcendentals=pairs),
        name="far_ahead",
    )(own, part, *blocks)


def stack(own, after, blocks):
    vmem = pl.BlockSpec(memory_space=pltpu.VMEM)
    return pl.pallas_call(
        stack_kernel,
        out_shape=jax.ShapeDtypeStruct((USED * (len(blocks) + 1), own.shape[1]), F32),
        in_specs=[vmem, pl.BlockSpec(memory_space=pl.ANY)] + [vmem] * len(blocks),
        out_specs=vmem,
        compiler_params=pltpu.CompilerParams(vmem_limit_bytes=VMEM_LIMIT),
        name="stack",
    )(own, after, *blocks)


def far_after(own, part, blocks):
    vmem = pl.BlockSpec(memory_space=pltpu.VMEM)
    pairs = (len(blocks) + 1) * own.shape[1] ** 2
    return pl.pallas_call(
        after_kernel,
        out_shape=jax.ShapeDtypeStruct(own.shape, F32),
        in_specs=[vmem] * (2 + len(blocks)),
        out_specs=vmem,
        compiler_params=pltpu.CompilerParams(vmem_limit_bytes=VMEM_LIMIT),
        cost_estimate=pl.CostEstimate(flops=PAIR_FLOPS * pairs, bytes_accessed=0, transcendentals=pairs),
        name="far_after",
    )(own, part, *blocks)


def flips(size, bit):
    return [(i, i ^ bit) for i in range(size)]


ORDER = (2, 3, 1)
LATER = (4, 8, 16, 32)


def shards(positions, density, upsample, cell_map, near_list):
    columns = lax.axis_size("blk")
    peers = lax.axis_size("nbr")
    own = jnp.concatenate([positions, density], axis=0)
    own, part = far_first(own)
    zs = [lax.ppermute(own, "blk", flips(columns, b)) for b in ORDER]
    tiles = near_panels(own, jnp.swapaxes(near_list, 1, 2), cell_map, upsample.shape[0], peers)
    near = [lax.ppermute(t, "nbr", flips(peers, d + 1)) for d, t in enumerate(tiles)]
    part = far_ahead(own, part, zs[:NEEDS])
    held = stack(own, part, zs)
    last = None
    for bit in LATER:
        if bit >= columns:
            break
        got = lax.ppermute(held, "blk", flips(columns, bit))
        if last is None:
            part = far_after(own, part, zs)
            part = pair_sums("near", own, part, [], near, upsample)
        else:
            part = pair_sums("far_%d" % bit, own, part, [last], [], upsample)
        held = jnp.concatenate([held, got])
        last = got
    return pair_sums("far_last", own, part, [last], [], upsample, final=True)


def solution(mesh):
    placed = (
        P(None, ("blk", "nbr")),
        P(None, ("blk", "nbr")),
        P(),
        P("blk", None),
        P(("blk", "nbr"), None, None),
    )
    return jax.shard_map(
        shards, mesh=mesh, in_specs=placed, out_specs=P(None, ("blk", "nbr")), check_vma=False
    )
```
